32 devices in a mesh: row: 8 (over y, x, core), col: 4 (over z).
Axes of the slice: x: 2, y: 2, z: 4, core: 2. Of those that a mesh axis runs over, the one named last changes fastest.
Arguments:
- a_panels: bfloat16 [8, 4, 16, 256, 256], P('row', 'col'), may hold values from -1.5 to 1.5
- b_panels: bfloat16 [8, 4, 16, 256, 256], P('row', 'col'), may hold values from -1.5 to 1.5
- a_rows: int32 [8, 4, 16], replicated, may hold values from 0 to 23, as said below
- a_inner: int32 [8, 4, 16], replicated, may hold values from 0 to 23, as said below
- b_inner: int32 [8, 4, 16], replicated, may hold values from 0 to 23, as said below
- b_cols: int32 [8, 4, 16], replicated, may hold values from 0 to 23, as said below
- c_rows: int32 [8, 4, 64], replicated, may hold values from 0 to 23, as said below
- c_cols: int32 [8, 4, 64], replicated, may hold values from 0 to 23
Outputs:
- c_blocks: bfloat16 [8, 4, 64, 256, 256], P('row', 'col')
The draws below stay inside these ranges and needn't reach their ends.
Inputs may be any that keep to these rules, and one draw needn't show every extreme that they name: `a_rows`: the blocks of one left panel stand at distinct positions; the left blocks and result blocks of one grid row use the same 8 block rows. `a_inner`: all left and right panels draw their inner indices from one common set of 8 indices, which holds 23; every left panel uses 24 - 1. `b_inner`: every right panel holds each index of the common set exactly twice. `b_cols`: the blocks of one right panel stand at distinct positions; the right blocks and result blocks of one grid column use the same 8 block columns. `c_rows`: the 64 result positions of one grid position are distinct and cover every pair of its grid row's block rows and its grid column's block columns.
All inputs are finite; a program needn't handle non-finite values.
Results may differ from the reference program's by a relative error of at most 0.001.
Values may be sent and summed in bfloat16 or wider, within the bound.
No kernel may reach another device: no remote copies, remote signals or barrier semaphores. Data moves between devices by JAX's collectives and lax.ppermute only.
A program may use at most 128 MiB of HBM per device.

```python
import jax
import jax.numpy as jnp
from jax import lax

BS = 256
PB = 24
RACT = 8
NBLK = 16
NC = 64
STEPS = 4
ROWS_GRID = 8
COLS_GRID = 4


def pattern(key):
    key = jax.random.fold_in(key, 23)
    row_key, col_key, left_key, right_key, result_key, common_key = jax.random.split(key, 6)
    half_count = NBLK // 2

    def active(subkey):
        return jax.random.permutation(subkey, PB)[:RACT].astype(jnp.int32)
    act_rows = jax.vmap(active)(jax.random.split(row_key, ROWS_GRID))
    act_cols = jax.vmap(active)(jax.random.split(col_key, COLS_GRID))
    common_head = jax.random.permutation(common_key, PB - 1)[:half_count - 1].astype(jnp.int32)
    common_set = jnp.concatenate([common_head, jnp.full((1,), PB - 1, jnp.int32)])
    devices = jnp.arange(ROWS_GRID * COLS_GRID, dtype=jnp.int32)
    grid_rows = devices // COLS_GRID
    grid_cols = devices % COLS_GRID

    def left_one(subkey, grid_row):
        keys_two = jax.random.split(subkey, 2)
        forced_row = jax.random.randint(keys_two[0], (1,), 0, RACT, dtype=jnp.int32)
        forced = forced_row * half_count + (half_count - 1)
        others = jax.random.permutation(keys_two[1], RACT * half_count - 1)[:NBLK - 1].astype(jnp.int32)
        others = jnp.where(others >= forced[0], others + 1, others)
        chosen = jnp.concatenate([forced, others]).astype(jnp.int32)
        return (act_rows[grid_row][chosen // half_count], common_set[chosen % half_count])

    def right_one(subkey, grid_col):
        subkeys = jax.random.split(subkey, 3)
        order = jax.random.permutation(subkeys[0], half_count).astype(jnp.int32)
        first_col = jax.random.randint(subkeys[1], (half_count,), 0, RACT, dtype=jnp.int32)
        offsets = jax.random.randint(subkeys[2], (half_count,), 1, RACT, dtype=jnp.int32)
        second_col = (first_col + offsets) % RACT
        inner_index = jnp.concatenate([common_set, common_set[order]])
        column_index = jnp.concatenate([first_col, second_col[order]])
        return (inner_index, act_cols[grid_col][column_index])

    def result_one(subkey, grid_row, grid_col):
        chosen = jax.random.permutation(subkey, RACT * RACT)[:NC].astype(jnp.int32)
        return (act_rows[grid_row][chosen // RACT], act_cols[grid_col][chosen % RACT])
    total = ROWS_GRID * COLS_GRID
    left_rows, left_inner = jax.vmap(left_one)(jax.random.split(left_key, total), grid_rows)
    right_inner, right_cols = jax.vmap(right_one)(jax.random.split(right_key, total), grid_cols)
    result_rows, result_cols = jax.vmap(result_one)(jax.random.split(result_key, total), grid_rows, grid_cols)
    shaped = [left_rows, left_inner, right_inner, right_cols, result_rows, result_cols]
    return [jnp.reshape(entry, (ROWS_GRID, COLS_GRID, -1)).astype(jnp.int32) for entry in shaped]


def draw_a_rows(key, part):
    return pattern(key)[0]


def draw_a_inner(key, part):
    return pattern(key)[1]


def draw_b_inner(key, part):
    return pattern(key)[2]


def draw_b_cols(key, part):
    return pattern(key)[3]


def draw_c_rows(key, part):
    return pattern(key)[4]


def draw_c_cols(key, part):
    return pattern(key)[5]


def shard_levels(key, extent, pieces, low, top_value):
    factor_of, own = 1.0, jax.random.fold_in(key, 6)
    for position, blocks in pieces:
        draws = jnp.exp(jax.random.uniform(jax.random.fold_in(own, position), (blocks,), jnp.float32, low / len(pieces), top_value / len(pieces)))
        factor_of = factor_of * jnp.repeat(draws, extent[position] // blocks).reshape([-1 if axis == position else 1 for axis in range(len(extent))])
    return factor_of


def scatter_about(stream_key, shape, spread, most, pieces=(), kind=jnp.bfloat16):
    values = spread * jax.random.normal(stream_key, shape, jnp.float32)
    if pieces:
        values = values * shard_levels(stream_key, shape, pieces, -0.22, 0.18)
    return jnp.clip(values, -most, most).astype(kind)


def setup_inputs(seed: int = 0) -> dict:
    keys = jax.random.split(jax.random.key(seed), 9)
    return {
        "a_panels": scatter_about(keys[0], (ROWS_GRID, COLS_GRID, NBLK, BS, BS), 0.25, 1.5, ((0, 8), (1, 4))),
        "b_panels": scatter_about(keys[1], (ROWS_GRID, COLS_GRID, NBLK, BS, BS), 0.25, 1.5, ((0, 8), (1, 4))),
        "a_rows": draw_a_rows(jax.random.fold_in(keys[8], 71), 0),
        "a_inner": draw_a_inner(jax.random.fold_in(keys[8], 71), 0),
        "b_inner": draw_b_inner(jax.random.fold_in(keys[8], 71), 0),
        "b_cols": draw_b_cols(jax.random.fold_in(keys[8], 71), 0),
        "c_rows": draw_c_rows(jax.random.fold_in(keys[8], 71), 0),
        "c_cols": draw_c_cols(jax.random.fold_in(keys[8], 71), 0),
    }


def pick_pairs(left_inner, right_inner):
    count = right_inner.shape[0]
    places = jnp.arange(count, dtype=jnp.int32)
    matches = left_inner[:, None] == right_inner[None, :]
    first_pick = jnp.min(jnp.where(matches, places[None, :], count), axis=1)
    later = matches & (places[None, :] > first_pick[:, None])
    second_pick = jnp.min(jnp.where(later, places[None, :], count), axis=1)
    right_pick = jnp.stack([first_pick, second_pick], axis=1).reshape(-1).astype(jnp.int32)
    left_pick = jnp.repeat(jnp.arange(left_inner.shape[0], dtype=jnp.int32), 2)
    usable = right_pick < count
    return left_pick, jnp.minimum(right_pick, count - 1), usable


def target_slots(left_rows, right_cols, own_rows, own_cols, usable):
    slot_count = own_rows.shape[0]
    hit_table = (left_rows[:, None] == own_rows[None, :]) & (right_cols[:, None] == own_cols[None, :])
    places = jnp.arange(slot_count, dtype=jnp.int32)
    found_slot = jnp.min(jnp.where(hit_table, places[None, :], slot_count), axis=1)
    return jnp.where(usable, found_slot, slot_count).astype(jnp.int32)


def reference(a_panels, b_panels, a_rows, a_inner, b_inner, b_cols, c_rows, c_cols):
    def one_device(device):
        row_id = device // COLS_GRID
        col_id = device % COLS_GRID
        totals = jnp.zeros((NC, BS, BS), jnp.float32)
        for shift_step in range(STEPS):
            left_col = (col_id + shift_step) % COLS_GRID
            right_row = (row_id + shift_step) % ROWS_GRID
            left_blocks = a_panels[row_id, left_col]
            right_blocks = b_panels[right_row, col_id]
            left_pick, right_pick, usable = pick_pairs(a_inner[row_id, left_col], b_inner[right_row, col_id])
            slots = target_slots(a_rows[row_id, left_col][left_pick], b_cols[right_row, col_id][right_pick],
                                 c_rows[row_id, col_id], c_cols[row_id, col_id], usable)
            products = jnp.einsum("pik,pkj->pij", left_blocks[left_pick].astype(jnp.float32),
                                  right_blocks[right_pick].astype(jnp.float32))
            totals = totals.at[slots].add(products, mode="drop")
        return totals.astype(jnp.bfloat16)

    result = lax.map(one_device, jnp.arange(ROWS_GRID * COLS_GRID, dtype=jnp.int32))
    return result.reshape(ROWS_GRID, COLS_GRID, NC, BS, BS)
```

```python
import functools

import jax
import jax.numpy as jnp
from jax import lax
from jax.experimental import pallas as pl
from jax.experimental.pallas import tpu as pltpu
from jax.sharding import PartitionSpec as P

STEPS = 4
MAIN_VMEM = 52 * 2**20
PIECE_VMEM = 24 * 2**20


def shifted(value, axis, steps):
    count = lax.axis_size(axis)
    pairs = [(source, (source + steps) % count) for source in range(count)]
    return lax.ppermute(value, axis, pairs)


def main_kernel(routes, pieces, flag_ref, pick_ref, slot_ref, *refs):
    count = len(pieces)
    sources, refs = refs[: len(routes)], refs[len(routes) :]
    rights, refs = refs[: 2 * STEPS], refs[2 * STEPS :]
    out_ref, part_refs, held_refs = refs[0], refs[1 : 1 + count], refs[1 + count : 1 + 2 * count]
    lefts, right_all, totals, staged, left_sem, right_sem, out_sem, part_sem, held_sem = refs[
        1 + 2 * count :
    ]
    blocks = rights[0].shape[0]
    slots = totals.shape[0]
    flag, odd = flag_ref[0], flag_ref[1]

    def left_copy(place):
        _, start, size, _ = routes[place]
        return pltpu.make_async_copy(
            sources[place], lefts.at[pl.ds(start, size)], left_sem.at[place]
        )

    def when_used(place, action):
        wanted = routes[place][3]
        if wanted is None:
            action()
        else:
            pl.when(flag == wanted)(action)

    def right_copy(step, side):
        return pltpu.make_async_copy(
            rights[2 * step + side],
            right_all.at[pl.ds(step * blocks, blocks)],
            right_sem.at[step],
        )

    for step in range(STEPS):
        for side in range(2):
            pl.when(odd == side)(right_copy(step, side).start)
        for place, route in enumerate(routes):
            if route[0] == step:
                when_used(place, lambda place=place: left_copy(place).start())

    @pl.loop(0, slots)
    def _(slot):
        totals[slot] = jnp.zeros(totals.shape[1:], totals.dtype)

    for step in range(STEPS):
        right_copy(step, 0).wait()

    first_held = 2 * (STEPS - 1) * blocks
    tails = []
    for piece, size in enumerate(pieces):
        tails += [(piece, place) for place in range(2 * size)]

    def held_copy(pair):
        piece, place = tails[pair]
        return pltpu.make_async_copy(
            right_all.at[pick_ref[first_held + pair]],
            held_refs[piece].at[place],
            held_sem.at[pair],
        )

    def part_copy(pair):
        piece, place = tails[pair]
        return pltpu.make_async_copy(
            totals.at[slot_ref[first_held + pair]],
            part_refs[piece].at[place],
            part_sem.at[pair],
        )

    def out_copy(slot):
        return pltpu.make_async_copy(staged.at[slot], out_ref.at[slot], out_sem.at[slot])

    for pair in range(len(tails)):
        held_copy(pair).start()
    for step in range(STEPS - 1):
        for place, route in enumerate(routes):
            if route[0] == step:
                when_used(place, lambda place=place: left_copy(place).wait())

        @pl.loop(step * blocks, (step + 1) * blocks)
        def _(left):
            for side in range(2):
                totals[slot_ref[2 * left + side]] += jnp.dot(
                    lefts[left],
                    right_all[pick_ref[2 * left + side]],
                    preferred_element_type=jnp.float32,
                )

    for pair in range(len(tails)):
        part_copy(pair).start()

    @pl.loop(0, slots)
    def _(slot):
        staged[slot] = totals[slot].astype(staged.dtype)
        out_copy(slot).start()

    @pl.loop(0, slots)
    def _(slot):
        out_copy(slot).wait()

    for pair in range(len(tails)):
        part_copy(pair).wait()
        held_copy(pair).wait()


def main_call(routes, pieces, flag, picks, slots, sources, rights, slot_count):
    rights = [value for pair in rights for value in pair]
    blocks, width = rights[0].shape[0], rights[0].shape[1]
    dtype = rights[0].dtype
    smem = pl.BlockSpec(memory_space=pltpu.SMEM)
    hbm = pl.BlockSpec(memory_space=pl.ANY)
    kept = (STEPS - 1) * blocks
    result = pl.pallas_call(
        functools.partial(main_kernel, routes, pieces),
        out_shape=(
            jax.ShapeDtypeStruct((slot_count, width, width), dtype),
            *[jax.ShapeDtypeStruct((2 * size, width, width), jnp.float32) for size in pieces],
            *[jax.ShapeDtypeStruct((2 * size, width, width), dtype) for size in pieces],
        ),
        in_specs=[smem] * 3 + [hbm] * (len(sources) + 2 * STEPS),
        out_specs=(hbm,) * (1 + 2 * len(pieces)),
        scratch_shapes=[
            pltpu.VMEM((kept, width, width), dtype),
            pltpu.VMEM((STEPS * blocks, width, width), dtype),
            pltpu.VMEM((slot_count, width, width), jnp.float32),
            pltpu.VMEM((slot_count, width, width), dtype),
            pltpu.SemaphoreType.DMA((len(sources),)),
            pltpu.SemaphoreType.DMA((STEPS,)),
            pltpu.SemaphoreType.DMA((slot_count,)),
            pltpu.SemaphoreType.DMA((2 * blocks,)),
            pltpu.SemaphoreType.DMA((2 * blocks,)),
        ],
        compiler_params=pltpu.CompilerParams(vmem_limit_bytes=MAIN_VMEM),
        cost_estimate=pl.CostEstimate(
            flops=4 * kept * width**3,
            bytes_accessed=2 * width * width * (2 * STEPS * blocks + slot_count + 6 * blocks),
            transcendentals=0,
        ),
        name="first_panels",
    )(flag, picks, slots, *sources, *rights)
    return result[0], list(result[1 : 1 + len(pieces)]), list(result[1 + len(pieces) :])


def piece_kernel(choices, later, flag_ref, slot_ref, lead_ref, link_ref, *refs):
    lasts, refs = refs[:choices], refs[choices:]
    part_hbm, held_hbm, refs = refs[0], refs[1], refs[3 + len(later) :]
    out_ref, later_refs, refs = refs[0], refs[1 : 1 + len(later)], refs[1 + len(later) :]
    left, part, held, staged, in_sem, out_sem, later_sem = refs
    pairs = part.shape[0]
    held_copy = pltpu.make_async_copy(held_hbm, held, in_sem.at[0])
    part_copy = pltpu.make_async_copy(part_hbm, part, in_sem.at[1])
    left_copies = [pltpu.make_async_copy(last, left, in_sem.at[2]) for last in lasts]
    for place, copy in enumerate(left_copies):
        pl.when(flag_ref[0] == place)(copy.start)
    held_copy.start()
    part_copy.start()
    left_copies[0].wait()
    held_copy.wait()
    part_copy.wait()
    for pair in range(pairs):
        part[lead_ref[pair]] += jnp.dot(
            left[pair // 2], held[pair], preferred_element_type=jnp.float32
        )

    def out_copy(pair):
        return pltpu.make_async_copy(
            staged.at[pair], out_ref.at[slot_ref[pair]], out_sem.at[pair]
        )

    tails = []
    for piece, size in enumerate(later):
        tails += [(piece, place) for place in range(2 * size)]

    def later_copy(pair):
        piece, place = tails[pair]
        return pltpu.make_async_copy(
            part.at[link_ref[pair]], later_refs[piece].at[place], later_sem.at[pair]
        )

    for pair in range(pairs):

        @pl.when(lead_ref[pair] == pair)
        def _():
            staged[pair] = part[pair].astype(staged.dtype)
            out_copy(pair).start()

    for pair in range(len(tails)):
        pl.when(link_ref[pair] >= 0)(lambda pair=pair: later_copy(pair).start())
    for pair in range(pairs):
        pl.when(lead_ref[pair] == pair)(lambda pair=pair: out_copy(pair).wait())
    for pair in range(len(tails)):
        pl.when(link_ref[pair] >= 0)(lambda pair=pair: later_copy(pair).wait())


def piece_call(flag, slots, leads, links, lasts, part, held, out, later_parts):
    smem = pl.BlockSpec(memory_space=pltpu.SMEM)
    hbm = pl.BlockSpec(memory_space=pl.ANY)
    pairs, width = held.shape[0], held.shape[1]
    later = [value.shape[0] // 2 for value in later_parts]
    first_alias = 4 + len(lasts) + 2
    result = pl.pallas_call(
        functools.partial(piece_kernel, len(lasts), later),
        out_shape=tuple(
            jax.ShapeDtypeStruct(value.shape, value.dtype) for value in (out, *later_parts)
        ),
        in_specs=[smem] * 4 + [hbm] * (len(lasts) + 3 + len(later)),
        out_specs=(hbm,) * (1 + len(later)),
        input_output_aliases={first_alias + place: place for place in range(1 + len(later))},
        scratch_shapes=[
            pltpu.VMEM(lasts[0].shape, lasts[0].dtype),
            pltpu.VMEM(part.shape, part.dtype),
            pltpu.VMEM(held.shape, held.dtype),
            pltpu.VMEM(held.shape, held.dtype),
            pltpu.SemaphoreType.DMA((3,)),
            pltpu.SemaphoreType.DMA((pairs,)),
            pltpu.SemaphoreType.DMA((max(1, 2 * sum(later)),)),
        ],
        compiler_params=pltpu.CompilerParams(vmem_limit_bytes=PIECE_VMEM),
        cost_estimate=pl.CostEstimate(
            flops=2 * pairs * width**3,
            bytes_accessed=2 * width * width * 5 * pairs,
            transcendentals=0,
        ),
        name="last_panel_piece",
    )(flag, slots, leads, links, *lasts, part, held, out, *later_parts)
    return result[0], list(result[1:])


def cut(value, sizes):
    starts = [sum(sizes[:place]) for place in range(len(sizes))]
    return [value[start : start + size] for start, size in zip(starts, sizes)]


def after(value, *others):
    return lax.optimization_barrier((value, *others))[0]


def line_of_four(left, far_sizes):
    me = lax.axis_index("col")
    blocks = left.shape[0]
    cross, out = [(1, 2), (2, 1)], [(2, 3), (1, 0)]
    near = lax.ppermute(left, "col", [(0, 1), (1, 0), (2, 3), (3, 2)])
    mid_in = lax.ppermute(left, "col", cross)
    mid_out = lax.ppermute(mid_in, "col", out)
    far_in = [lax.ppermute(piece, "col", cross) for piece in cut(near, far_sizes)]
    far_out = [lax.ppermute(piece, "col", out) for piece in far_in]
    low = me < 2
    columns = jnp.stack([me, me ^ 1, jnp.where(low, 2, 1), jnp.where(low, 3, 0)])
    at_end = (me == 0) | (me == 3)
    routes = [(0, 0, blocks, None), (1, blocks, blocks, None)]
    routes += [(2, 2 * blocks, blocks, 0), (2, 2 * blocks, blocks, 1)]
    arrays = [left, near, mid_in, mid_out]
    return columns, routes, arrays, list(zip(far_in, far_out)), at_end


def ring(left, far_sizes):
    me, count = lax.axis_index("col"), lax.axis_size("col")
    blocks = left.shape[0]
    near = shifted(left, "col", -1)
    mid = shifted(near, "col", -1)
    far = [shifted(piece, "col", -1) for piece in cut(mid, far_sizes)]
    columns = (me + jnp.arange(STEPS, dtype=jnp.int32)) % count
    routes = [(step, step * blocks, blocks, None) for step in range(STEPS - 1)]
    return columns, routes, [left, near, mid], [(piece,) for piece in far], me < 0


def right_panels(right, behind):
    count = lax.axis_size("row")
    own = lax.ppermute(right, "row", [(row + 1, row) for row in range(0, count, 2)])
    two = shifted(right, "row", -2)
    three = lax.ppermute(
        right, "row", [((row + 3) % count, row) for row in range(1, count, 2)]
    )
    swapped = lax.ppermute(after(two, behind), "row", [(row, row ^ 1) for row in range(count)])
    return [(own, swapped), (two, two), (swapped, three)]


def pair_tables(columns, a_rows, a_inner, b_inner, b_cols, own_rows, own_cols):
    row_id, col_id = lax.axis_index("row"), lax.axis_index("col")
    row_count, col_count = lax.axis_size("row"), lax.axis_size("col")
    steps = (columns - col_id + col_count) % col_count
    left_rows, left_inner = a_rows[row_id][columns], a_inner[row_id][columns]
    right_rows = (row_id + steps) % row_count
    right_inner = b_inner[:, col_id][right_rows]
    right_cols = b_cols[:, col_id][right_rows]
    count = right_inner.shape[1]
    places = jnp.arange(count, dtype=jnp.int32)
    matches = left_inner[:, :, None] == right_inner[:, None, :]
    first = jnp.min(jnp.where(matches, places, count - 1), axis=2)
    second = jnp.max(jnp.where(matches, places, 0), axis=2)
    picks = jnp.stack([first, second], axis=2)
    pair_cols = jnp.sum(
        jnp.where(picks[..., None] == places, right_cols[:, None, None, :], 0), axis=3
    )
    hits = (left_rows[:, :, None, None] == own_rows) & (pair_cols[..., None] == own_cols)
    slot_places = jnp.arange(own_rows.shape[0], dtype=jnp.int32)
    slots = jnp.sum(jnp.where(hits, slot_places, 0), axis=3)
    picks = picks + (steps * count)[:, None, None]
    return picks.reshape(-1).astype(jnp.int32), slots.reshape(-1).astype(jnp.int32)


def on_device(a_panels, b_panels, a_rows, a_inner, b_inner, b_cols, c_rows, c_cols):
    row_id, col_id = lax.axis_index("row"), lax.axis_index("col")
    left, right = a_panels[0, 0], b_panels[0, 0]
    own_rows, own_cols = c_rows[row_id, col_id], c_cols[row_id, col_id]
    gather = line_of_four if lax.axis_size("col") == STEPS else ring
    quarter = left.shape[0] // 4
    rest = left.shape[0] - quarter
    far_sizes = (rest - quarter, quarter, quarter)
    columns, routes, sources, lasts, at_end = gather(left, far_sizes)
    rights = [(right, right), *right_panels(right, lasts[0][0])]
    picks, slots = pair_tables(columns, a_rows, a_inner, b_inner, b_cols, own_rows, own_cols)
    flag = jnp.stack([at_end.astype(jnp.int32), row_id % 2])
    out, parts, helds = main_call(
        routes, far_sizes, flag, picks, slots, sources, rights, c_rows.shape[2]
    )
    piece_slots = cut(slots[-2 * left.shape[0] :], [2 * size for size in far_sizes])
    for place, here in enumerate(piece_slots):
        places = jnp.arange(here.shape[0], dtype=jnp.int32)

        def lead(wanted, other):
            found = jnp.where(wanted[:, None] == here[None, :], places[None, :], here.shape[0])
            first = jnp.min(found, axis=1)
            return jnp.where(first < here.shape[0], first, other)

        leads = lead(here, 0)
        links = lead(jnp.concatenate([*piece_slots[place + 1 :], here[:1]]), -1)
        out, later = piece_call(
            flag, here, leads, links, lasts[place], parts[place], helds[place], out, parts[place + 1 :]
        )
        parts[place + 1 :] = later
    return out[None, None]


def solution(mesh):
    in_specs = (
        P("row", "col", None, None, None),
        P("row", "col", None, None, None),
        P(),
        P(),
        P(),
        P(),
        P(),
        P(),
    )
    out_specs = P("row", "col", None, None, None)
    return jax.shard_map(
        on_device, mesh=mesh, in_specs=in_specs, out_specs=out_specs, check_vma=False
    )
```

```python
import functools

import jax
import jax.numpy as jnp
from jax import lax
from jax.experimental import pallas as pl
from jax.experimental.pallas import tpu as pltpu
from jax.sharding import PartitionSpec as P

STEPS = 4
VMEM_BYTES = 60 * 2**20
FINAL_VMEM = 16 * 2**20
UNROLL = 4
SMALL = pl.CostEstimate(flops=2**20, bytes_accessed=2**16, transcendentals=0)


def shifted(value, axis, steps):
    count = lax.axis_size(axis)
    pairs = [(source, (source + steps) % count) for source in range(count)]
    return lax.ppermute(value, axis, pairs)


def main_kernel(routes, takers, pieces, layout, table_ref, *refs):
    count = len(pieces)
    sources, refs = refs[: len(routes)], refs[len(routes) :]
    rights, refs = refs[: len(takers)], refs[len(takers) :]
    out_ref, part_refs, held_refs = refs[0], refs[1 : 1 + count], refs[1 + count : 1 + 2 * count]
    lefts, right_all, totals, staged, left_sem, right_sem, out_sem, part_sem, held_sem = refs[
        1 + 2 * count :
    ]
    blocks = rights[0].shape[0]
    slots = totals.shape[0]
    flag, kind = table_ref[layout["flags"]], table_ref[layout["flags"] + 1]

    def pick_of(pair):
        return table_ref[layout["picks"] + pair]

    def slot_of(pair):
        return table_ref[layout["slots"] + pair]

    def left_copy(place):
        _, start, size, _ = routes[place]
        return pltpu.make_async_copy(
            sources[place], lefts.at[pl.ds(start, size)], left_sem.at[place]
        )

    def when_used(place, action):
        wanted = routes[place][3]
        if wanted is None:
            action()
        else:
            pl.when(flag == wanted)(action)

    def right_copy(place):
        step, start, _ = takers[place]
        return pltpu.make_async_copy(
            rights[place],
            right_all.at[pl.ds(step * blocks + start, rights[place].shape[0])],
            right_sem.at[place],
        )

    def when_taken(step, action):
        for place, (wanted, _, kinds) in enumerate(takers):
            if wanted == step:
                for one in kinds:
                    pl.when(kind == one)(lambda place=place: action(place))

    for step in range(STEPS):
        for place, route in enumerate(routes):
            if route[0] == step:
                when_used(place, lambda place=place: left_copy(place).start())
        when_taken(step, lambda place: right_copy(place).start())

    @pl.loop(0, slots)
    def _(slot):
        totals[slot] = jnp.zeros(totals.shape[1:], totals.dtype)

    first_held = 2 * (STEPS - 1) * blocks
    tails = []
    for piece, size in enumerate(pieces):
        tails += [(piece, place) for place in range(2 * size)]

    def held_copy(pair):
        piece, place = tails[pair]
        return pltpu.make_async_copy(
            right_all.at[pick_of(first_held + pair)],
            held_refs[piece].at[place],
            held_sem.at[pair],
        )

    def part_copy(pair):
        piece, place = tails[pair]
        return pltpu.make_async_copy(
            totals.at[slot_of(first_held + pair)],
            part_refs[piece].at[place],
            part_sem.at[pair],
        )

    def out_copy(slot):
        return pltpu.make_async_copy(staged.at[slot], out_ref.at[slot], out_sem.at[slot])

    for step in range(STEPS - 1):
        for place, route in enumerate(routes):
            if route[0] == step:
                when_used(place, lambda place=place: left_copy(place).wait())
        for other in [(0,), range(1, STEPS), ()][min(step, 2)]:
            when_taken(other, lambda place: right_copy(place).wait())
        if step == 1:
            for pair in range(len(tails)):
                held_copy(pair).start()

        @pl.loop(step * blocks, (step + 1) * blocks, unroll=UNROLL)
        def _(left):
            for side in range(2):
                totals[slot_of(2 * left + side)] += jnp.dot(
                    lefts[left],
                    right_all[pick_of(2 * left + side)],
                    preferred_element_type=jnp.float32,
                )

    for pair in range(len(tails)):
        part_copy(pair).start()

    @pl.loop(0, slots)
    def _(slot):
        staged[slot] = totals[slot].astype(staged.dtype)
        out_copy(slot).start()

    @pl.loop(0, slots)
    def _(slot):
        out_copy(slot).wait()

    for pair in range(len(tails)):
        part_copy(pair).wait()
        held_copy(pair).wait()


def main_call(routes, takers, pieces, layout, table, sources, rights, slot_count):
    blocks, width = rights[0].shape[0], rights[0].shape[1]
    dtype = rights[0].dtype
    smem = pl.BlockSpec(memory_space=pltpu.SMEM)
    hbm = pl.BlockSpec(memory_space=pl.ANY)
    kept = (STEPS - 1) * blocks
    result = pl.pallas_call(
        functools.partial(main_kernel, routes, takers, pieces, layout),
        out_shape=(
            jax.ShapeDtypeStruct((slot_count, width, width), dtype),
            *[jax.ShapeDtypeStruct((2 * size, width, width), jnp.float32) for size in pieces],
            *[jax.ShapeDtypeStruct((2 * size, width, width), dtype) for size in pieces],
        ),
        in_specs=[smem] + [hbm] * (len(sources) + len(rights)),
        out_specs=(hbm,) * (1 + 2 * len(pieces)),
        scratch_shapes=[
            pltpu.VMEM((kept, width, width), dtype),
            pltpu.VMEM((STEPS * blocks, width, width), dtype),
            pltpu.VMEM((slot_count, width, width), jnp.float32),
            pltpu.VMEM((slot_count, width, width), dtype),
            pltpu.SemaphoreType.DMA((len(sources),)),
            pltpu.SemaphoreType.DMA((len(rights),)),
            pltpu.SemaphoreType.DMA((slot_count,)),
            pltpu.SemaphoreType.DMA((2 * blocks,)),
            pltpu.SemaphoreType.DMA((2 * blocks,)),
        ],
        compiler_params=pltpu.CompilerParams(vmem_limit_bytes=VMEM_BYTES),
        cost_estimate=SMALL,
        name="first_panels",
    )(table, *sources, *rights)
    return result[0], list(result[1 : 1 + len(pieces)]), list(result[1 + len(pieces) :])


def piece_kernel(choices, later, layout, number, table_ref, *refs):
    def entry(name, pair):
        return table_ref[layout[name, number] + pair]

    lasts, refs = refs[:choices], refs[choices:]
    part_hbm, held_hbm, refs = refs[0], refs[1], refs[3 + len(later) :]
    out_ref, later_refs, refs = refs[0], refs[1 : 1 + len(later)], refs[1 + len(later) :]
    left, part, held, staged, left_sem, held_sem, part_sem, out_sem, later_sem = refs
    pairs = part.shape[0]

    def left_copy(block, place):
        return pltpu.make_async_copy(
            lasts[place].at[block], left.at[block], left_sem.at[block]
        )

    def held_copy(pair):
        return pltpu.make_async_copy(held_hbm.at[pair], held.at[pair], held_sem.at[pair])

    def part_copy(pair):
        return pltpu.make_async_copy(part_hbm.at[pair], part.at[pair], part_sem.at[pair])

    def out_copy(pair):
        return pltpu.make_async_copy(
            staged.at[pair], out_ref.at[entry("here", pair)], out_sem.at[pair]
        )

    for block in range(pairs // 2):
        for place in range(choices):
            pl.when(table_ref[layout["flags"]] == place)(
                lambda block=block, place=place: left_copy(block, place).start()
            )
        for pair in (2 * block, 2 * block + 1):
            held_copy(pair).start()
            part_copy(pair).start()

    for pair in range(pairs):
        if pair % 2 == 0:
            left_copy(pair // 2, 0).wait()
        held_copy(pair).wait()
        part_copy(pair).wait()
        lead = entry("lead", pair)
        total = part[lead] + jnp.dot(
            left[pair // 2], held[pair], preferred_element_type=jnp.float32
        )
        part[lead] = total
        staged[pair] = total.astype(staged.dtype)
        pl.when(entry("final", pair) == 1)(lambda pair=pair: out_copy(pair).start())

    tails = []
    for piece, size in enumerate(later):
        tails += [(piece, place) for place in range(2 * size)]

    def later_copy(pair):
        piece, place = tails[pair]
        return pltpu.make_async_copy(
            part.at[entry("link", pair)], later_refs[piece].at[place], later_sem.at[pair]
        )

    for pair in range(len(tails)):
        pl.when(entry("link", pair) >= 0)(lambda pair=pair: later_copy(pair).start())
    for pair in range(pairs):
        pl.when(entry("final", pair) == 1)(lambda pair=pair: out_copy(pair).wait())
    for pair in range(len(tails)):
        pl.when(entry("link", pair) >= 0)(lambda pair=pair: later_copy(pair).wait())


def piece_call(layout, number, table, lasts, part, held, out, later_parts):
    smem = pl.BlockSpec(memory_space=pltpu.SMEM)
    hbm = pl.BlockSpec(memory_space=pl.ANY)
    pairs, width = held.shape[0], held.shape[1]
    later = [value.shape[0] // 2 for value in later_parts]
    first_alias = 1 + len(lasts) + 2
    result = pl.pallas_call(
        functools.partial(piece_kernel, len(lasts), later, layout, number),
        out_shape=tuple(
            jax.ShapeDtypeStruct(value.shape, value.dtype) for value in (out, *later_parts)
        ),
        in_specs=[smem] + [hbm] * (len(lasts) + 3 + len(later)),
        out_specs=(hbm,) * (1 + len(later)),
        input_output_aliases={first_alias + place: place for place in range(1 + len(later))},
        scratch_shapes=[
            pltpu.VMEM(lasts[0].shape, lasts[0].dtype),
            pltpu.VMEM(part.shape, part.dtype),
            pltpu.VMEM(held.shape, held.dtype),
            pltpu.VMEM(held.shape, held.dtype),
            pltpu.SemaphoreType.DMA((pairs // 2,)),
            pltpu.SemaphoreType.DMA((pairs,)),
            pltpu.SemaphoreType.DMA((pairs,)),
            pltpu.SemaphoreType.DMA((pairs,)),
            pltpu.SemaphoreType.DMA((max(1, 2 * sum(later)),)),
        ],
        compiler_params=pltpu.CompilerParams(vmem_limit_bytes=VMEM_BYTES),
        cost_estimate=SMALL,
        name="last_panel_piece",
    )(table, *lasts, part, held, out, *later_parts)
    return result[0], list(result[1:])


def final_kernel(choices, layout, number, table_ref, *refs):
    lasts, refs = refs[:choices], refs[choices:]
    part_hbm, held, _, out_ref, part, totals, staged, part_sem, out_sem = refs
    pairs = part.shape[0]
    part_copies = [
        pltpu.make_async_copy(part_hbm.at[pair], part.at[pair], part_sem.at[pair])
        for pair in range(pairs)
    ]
    for copy in part_copies:
        copy.start()

    def entry(name, pair):
        return table_ref[layout[name, number] + pair]

    def out_copy(pair):
        return pltpu.make_async_copy(
            staged.at[pair], out_ref.at[entry("here", pair)], out_sem.at[pair]
        )

    for block in range(pairs // 2):
        left = lasts[0][block]
        for place in range(1, choices):
            left = jnp.where(table_ref[layout["flags"]] == place, lasts[place][block], left)
        for pair in (2 * block, 2 * block + 1):
            lead = entry("lead", pair)
            product = jnp.dot(left, held[pair], preferred_element_type=jnp.float32)
            part_copies[pair].wait()

            @pl.when(lead == pair)
            def _():
                totals[pair] = part[pair] + product

            @pl.when(lead != pair)
            def _():
                totals[lead] += product

            @pl.when(entry("final", pair) == 1)
            def _():
                staged[pair] = totals[lead].astype(staged.dtype)
                out_copy(pair).start()

    for pair in range(pairs):
        pl.when(entry("final", pair) == 1)(lambda pair=pair: out_copy(pair).wait())


def final_call(layout, number, table, lasts, part, held, out):
    smem = pl.BlockSpec(memory_space=pltpu.SMEM)
    vmem = pl.BlockSpec(memory_space=pltpu.VMEM)
    hbm = pl.BlockSpec(memory_space=pl.ANY)
    pinned = pl.BlockSpec(memory_space=pltpu.HBM)
    pairs, width = held.shape[0], held.shape[1]
    return pl.pallas_call(
        functools.partial(final_kernel, len(lasts), layout, number),
        out_shape=jax.ShapeDtypeStruct(out.shape, out.dtype),
        in_specs=[smem] + [vmem] * len(lasts) + [pinned, vmem, hbm],
        out_specs=hbm,
        input_output_aliases={len(lasts) + 3: 0},
        scratch_shapes=[
            pltpu.VMEM(part.shape, part.dtype),
            pltpu.VMEM(part.shape, part.dtype),
            pltpu.VMEM(held.shape, held.dtype),
            pltpu.SemaphoreType.DMA((pairs,)),
            pltpu.SemaphoreType.DMA((pairs,)),
        ],
        compiler_params=pltpu.CompilerParams(vmem_limit_bytes=FINAL_VMEM),
        cost_estimate=SMALL,
        name="last_piece",
    )(table, *lasts, part, held, out)


def cut(value, sizes):
    starts = [sum(sizes[:place]) for place in range(len(sizes))]
    return [value[start : start + size] for start, size in zip(starts, sizes)]


def after(value, *others):
    return lax.optimization_barrier((value, *others))[0]


def line_columns(me):
    low = me < 2
    return jnp.stack([me, me ^ 1, jnp.where(low, 2, 1), jnp.where(low, 3, 0)])


def ring_columns(me):
    return (me + jnp.arange(STEPS, dtype=jnp.int32)) % lax.axis_size("col")


def line_of_four(left, far_sizes, early, fetched):
    blocks = left.shape[0]
    cross, out = [(1, 2), (2, 1)], [(2, 3), (1, 0)]
    near = lax.ppermute(left, "col", [(0, 1), (1, 0), (2, 3), (3, 2)])
    mid_in = lax.ppermute(left, "col", cross)
    mid_out = lax.ppermute(mid_in, "col", out)
    near = after(near, mid_in, early)
    far_in = [
        lax.ppermute(after(piece, *fetched) if place == 1 else piece, "col", cross)
        for place, piece in enumerate(cut(near, far_sizes))
    ]
    far_out = [
        lax.ppermute(after(piece, mid_out) if place else piece, "col", out)
        for place, piece in enumerate(far_in)
    ]
    routes = [(0, 0, blocks, None), (1, blocks, blocks, None)]
    routes += [(2, 2 * blocks, blocks, 0), (2, 2 * blocks, blocks, 1)]
    return routes, [left, near, mid_in, mid_out], list(zip(far_in, far_out))


def ring(left, far_sizes, *_):
    blocks = left.shape[0]
    near = shifted(left, "col", -1)
    mid = shifted(near, "col", -1)
    far = [shifted(piece, "col", -1) for piece in cut(mid, far_sizes)]
    routes = [(step, step * blocks, blocks, None) for step in range(STEPS - 1)]
    return routes, [left, near, mid], [(piece,) for piece in far]


def right_panels(right):
    count = lax.axis_size("row")
    rows = range(count)

    def send(value, takers, distance):
        pairs = [((row + distance) % count, row) for row in rows if row % 4 in takers]
        return lax.ppermute(value, "row", pairs)

    own = send(right, (0, 2), 1)
    two = send(right, (0, 1, 2, 3), 2)
    three = send(right, (1, 3), 3)
    return own, two, three


def passed_on(own, two, three):
    half = two.shape[0] // 2
    rows = range(lax.axis_size("row"))
    swap = [(row, row ^ 1) for row in rows]
    passed = [lax.ppermute(part, "row", swap) for part in (two[:half], two[half:])]
    takers = [(1, 0, (0, 2)), (2, 0, (0, 1, 2, 3)), (3, 0, (1, 3))]
    for place in range(2):
        takers += [(1, place * half, (1, 3)), (3, place * half, (0, 2))]
    return takers, [own, two, three, *[part for part in passed for _ in range(2)]]


def pair_tables(columns, a_rows, a_inner, b_inner, b_cols, own_rows, own_cols):
    row_id, col_id = lax.axis_index("row"), lax.axis_index("col")
    row_count, col_count = lax.axis_size("row"), lax.axis_size("col")
    steps = (columns - col_id + col_count) % col_count
    left_rows, left_inner = a_rows[row_id][columns], a_inner[row_id][columns]
    right_rows = (row_id + steps) % row_count
    right_inner = b_inner[:, col_id][right_rows]
    right_cols = b_cols[:, col_id][right_rows]
    count = right_inner.shape[1]
    places = jnp.arange(count, dtype=jnp.int32)
    matches = left_inner[:, :, None] == right_inner[:, None, :]
    first = jnp.min(jnp.where(matches, places, count - 1), axis=2)
    second = jnp.max(jnp.where(matches, places, 0), axis=2)
    picks = jnp.stack([first, second], axis=2)
    pair_cols = jnp.sum(
        jnp.where(picks[..., None] == places, right_cols[:, None, None, :], 0), axis=3
    )
    hits = (left_rows[:, :, None, None] == own_rows) & (pair_cols[..., None] == own_cols)
    slot_places = jnp.arange(own_rows.shape[0], dtype=jnp.int32)
    slots = jnp.sum(jnp.where(hits, slot_places, 0), axis=3)
    picks = picks + (steps * count)[:, None, None]
    return picks.reshape(-1).astype(jnp.int32), slots.reshape(-1).astype(jnp.int32)


def piece_tables(slots, sizes):
    cuts = cut(slots, [2 * size for size in sizes])
    tables = {}
    for number, here in enumerate(cuts):
        count = here.shape[0]
        places = jnp.arange(count, dtype=jnp.int32)

        def lead(wanted):
            same = wanted[:, None] == here[None, :]
            first = jnp.min(jnp.where(same, places[None, :], count), axis=1)
            return jnp.where(first < count, first, -1)

        again = (here[:, None] == here[None, :]) & (places[None, :] > places[:, None])
        tables["here", number] = here
        tables["lead", number] = lead(here)
        tables["final", number] = 1 - jnp.max(again.astype(jnp.int32), axis=1)
        if number + 1 < len(sizes):
            tables["link", number] = lead(jnp.concatenate(cuts[number + 1 :]))
    return tables


def packed(tables):
    starts, total = {}, 0
    for name, value in tables.items():
        starts[name], total = total, total + value.shape[0]
    return jnp.concatenate([value.astype(jnp.int32) for value in tables.values()]), starts


def on_device(a_panels, b_panels, a_rows, a_inner, b_inner, b_cols, c_rows, c_cols):
    row_id, col_id = lax.axis_index("row"), lax.axis_index("col")
    left, right = a_panels[0, 0], b_panels[0, 0]
    own_rows, own_cols = c_rows[row_id, col_id], c_cols[row_id, col_id]
    on_line = lax.axis_size("col") == STEPS
    eighth = left.shape[0] // 8
    far_sizes = (left.shape[0] - 4 * eighth, 3 * eighth, eighth)
    columns = (line_columns if on_line else ring_columns)(col_id)
    picks, slots = pair_tables(columns, a_rows, a_inner, b_inner, b_cols, own_rows, own_cols)
    at_end = on_line & ((col_id == 0) | (col_id == 3))
    flags = jnp.stack([at_end.astype(jnp.int32), row_id % 4])
    pieces = piece_tables(slots[-2 * left.shape[0] :], far_sizes)
    table, layout = packed({"flags": flags, "picks": picks, "slots": slots, **pieces})
    gather = line_of_four if on_line else ring
    fetched = right_panels(right)
    routes, sources, lasts = gather(left, far_sizes, table, fetched)
    takers, rights = passed_on(*fetched)
    out, parts, helds = main_call(
        routes,
        [(0, 0, (0, 1, 2, 3)), *takers],
        far_sizes,
        layout,
        table,
        sources,
        [right, *rights],
        c_rows.shape[2],
    )
    last = len(far_sizes) - 1
    for number in range(last):
        out, parts[number + 1 :] = piece_call(
            layout, number, table, lasts[number], parts[number], helds[number], out, parts[number + 1 :]
        )
    out = final_call(layout, last, table, lasts[last], parts[last], helds[last], out)
    return out[None, None]


def solution(mesh):
    in_specs = (
        P("row", "col", None, None, None),
        P("row", "col", None, None, None),
        P(),
        P(),
        P(),
        P(),
        P(),
        P(),
    )
    out_specs = P("row", "col", None, None, None)
    return jax.shard_map(
        on_device, mesh=mesh, in_specs=in_specs, out_specs=out_specs, check_vma=False
    )
```

```python
import functools

import jax
import jax.numpy as jnp
from jax import lax
from jax.experimental import pallas as pl
from jax.experimental.pallas import tpu as pltpu
from jax.sharding import PartitionSpec as P

STEPS = 4
VMEM_BYTES = 60 * 2**20
PIECE_VMEM = 40 * 2**20
FINAL_VMEM = 16 * 2**20
UNROLL = 4
SMALL = pl.CostEstimate(flops=2**20, bytes_accessed=2**16, transcendentals=0)


def shifted(value, axis, steps):
    count = lax.axis_size(axis)
    pairs = [(source, (source + steps) % count) for source in range(count)]
    return lax.ppermute(value, axis, pairs)


def main_kernel(routes, takers, pieces, layout, table_ref, *refs):
    count = len(pieces)
    sources, refs = refs[: len(routes)], refs[len(routes) :]
    rights, refs = refs[: len(takers)], refs[len(takers) :]
    out_ref, part_refs, held_refs = refs[0], refs[1 : 1 + count], refs[1 + count : 1 + 2 * count]
    lefts, right_all, totals, staged, left_sem, right_sem, out_sem, part_sem, held_sem = refs[
        1 + 2 * count :
    ]
    blocks = rights[0].shape[0]
    slots = totals.shape[0]
    flag, kind = table_ref[layout["flags"]], table_ref[layout["flags"] + 1]

    def pick_of(pair):
        return table_ref[layout["picks"] + pair]

    def slot_of(pair):
        return table_ref[layout["slots"] + pair]

    def left_copy(place):
        _, start, size, _ = routes[place]
        return pltpu.make_async_copy(
            sources[place], lefts.at[pl.ds(start, size)], left_sem.at[place]
        )

    def when_used(place, action):
        wanted = routes[place][3]
        if wanted is None:
            action()
        else:
            pl.when(flag == wanted)(action)

    def right_copy(place):
        step, start, _ = takers[place]
        return pltpu.make_async_copy(
            rights[place],
            right_all.at[pl.ds(step * blocks + start, rights[place].shape[0])],
            right_sem.at[place],
        )

    def when_taken(step, action):
        for place, (wanted, _, kinds) in enumerate(takers):
            if wanted == step:
                for one in kinds:
                    pl.when(kind == one)(lambda place=place: action(place))

    for step in range(STEPS):
        for place, route in enumerate(routes):
            if route[0] == step:
                when_used(place, lambda place=place: left_copy(place).start())
        when_taken(step, lambda place: right_copy(place).start())

    @pl.loop(0, slots)
    def _(slot):
        totals[slot] = jnp.zeros(totals.shape[1:], totals.dtype)

    first_held = 2 * (STEPS - 1) * blocks
    tails = []
    for piece, size in enumerate(pieces):
        tails += [(piece, place) for place in range(2 * size)]

    def held_copy(pair):
        piece, place = tails[pair]
        return pltpu.make_async_copy(
            right_all.at[pick_of(first_held + pair)],
            held_refs[piece].at[place],
            held_sem.at[pair],
        )

    def part_copy(pair):
        piece, place = tails[pair]
        return pltpu.make_async_copy(
            totals.at[slot_of(first_held + pair)],
            part_refs[piece].at[place],
            part_sem.at[pair],
        )

    def out_copy(slot):
        return pltpu.make_async_copy(staged.at[slot], out_ref.at[slot], out_sem.at[slot])

    for step in range(STEPS - 1):
        for place, route in enumerate(routes):
            if route[0] == step:
                when_used(place, lambda place=place: left_copy(place).wait())
        for other in [(0,), range(1, STEPS), ()][min(step, 2)]:
            when_taken(other, lambda place: right_copy(place).wait())
        if step == 1:
            for pair in range(len(tails)):
                held_copy(pair).start()

        @pl.loop(step * blocks, (step + 1) * blocks, unroll=UNROLL)
        def _(left):
            for side in range(2):
                totals[slot_of(2 * left + side)] += jnp.dot(
                    lefts[left],
                    right_all[pick_of(2 * left + side)],
                    preferred_element_type=jnp.float32,
                )

    for pair in range(len(tails)):
        part_copy(pair).start()

    @pl.loop(0, slots)
    def _(slot):
        staged[slot] = totals[slot].astype(staged.dtype)
        out_copy(slot).start()

    @pl.loop(0, slots)
    def _(slot):
        out_copy(slot).wait()

    for pair in range(len(tails)):
        part_copy(pair).wait()
        held_copy(pair).wait()


def main_call(routes, takers, pieces, layout, table, sources, rights, slot_count):
    blocks, width = rights[0].shape[0], rights[0].shape[1]
    dtype = rights[0].dtype
    smem = pl.BlockSpec(memory_space=pltpu.SMEM)
    hbm = pl.BlockSpec(memory_space=pl.ANY)
    kept = (STEPS - 1) * blocks
    result = pl.pallas_call(
        functools.partial(main_kernel, routes, takers, pieces, layout),
        out_shape=(
            jax.ShapeDtypeStruct((slot_count, width, width), dtype),
            *[jax.ShapeDtypeStruct((2 * size, width, width), jnp.float32) for size in pieces],
            *[jax.ShapeDtypeStruct((2 * size, width, width), dtype) for size in pieces],
        ),
        in_specs=[smem] + [hbm] * (len(sources) + len(rights)),
        out_specs=(hbm,) * (1 + 2 * len(pieces)),
        scratch_shapes=[
            pltpu.VMEM((kept, width, width), dtype),
            pltpu.VMEM((STEPS * blocks, width, width), dtype),
            pltpu.VMEM((slot_count, width, width), jnp.float32),
            pltpu.VMEM((slot_count, width, width), dtype),
            pltpu.SemaphoreType.DMA((len(sources),)),
            pltpu.SemaphoreType.DMA((len(rights),)),
            pltpu.SemaphoreType.DMA((slot_count,)),
            pltpu.SemaphoreType.DMA((2 * blocks,)),
            pltpu.SemaphoreType.DMA((2 * blocks,)),
        ],
        compiler_params=pltpu.CompilerParams(vmem_limit_bytes=VMEM_BYTES),
        cost_estimate=SMALL,
        name="first_panels",
    )(table, *sources, *rights)
    return result[0], list(result[1 : 1 + len(pieces)]), list(result[1 + len(pieces) :])


def piece_kernel(choices, later, fresh, layout, number, table_ref, *refs):
    def entry(name, pair):
        return table_ref[layout[name, number] + pair]

    lasts, refs = refs[:choices], refs[choices:]
    part_hbm, held_hbm, before, refs = refs[0], refs[1], refs[3 : 3 + len(later)], refs[3 + len(later) :]
    out_ref, later_refs, refs = refs[0], refs[1 : 1 + len(later)], refs[1 + len(later) :]
    left, part, held, products, staged, in_sem, out_sem, later_sem = refs
    pairs = part.shape[0]

    left_copies = [pltpu.make_async_copy(last, left, in_sem.at[0]) for last in lasts]
    held_copy = pltpu.make_async_copy(held_hbm, held, in_sem.at[1])
    part_copy = pltpu.make_async_copy(part_hbm, part, in_sem.at[2])

    def out_copy(pair):
        return pltpu.make_async_copy(
            staged.at[pair], out_ref.at[entry("here", pair)], out_sem.at[pair]
        )

    held_copy.start()
    part_copy.start()
    for place, copy in enumerate(left_copies):
        pl.when(table_ref[layout["flags"]] == place)(copy.start)
    left_copies[0].wait()
    held_copy.wait()
    for pair in range(pairs):
        products[pair] = jnp.dot(
            left[pair // 2], held[pair], preferred_element_type=jnp.float32
        )
    part_copy.wait()
    for pair in range(pairs):
        part[entry("lead", pair)] += products[pair]
    for pair in range(pairs):
        staged[pair] = part[entry("lead", pair)].astype(staged.dtype)
        pl.when(entry("final", pair) == 1)(lambda pair=pair: out_copy(pair).start())

    tails = []
    for piece, size in enumerate(later):
        tails += [(piece, place) for place in range(2 * size)]

    def later_copy(pair):
        piece, place = tails[pair]
        return pltpu.make_async_copy(
            part.at[entry("link", pair)], later_refs[piece].at[place], later_sem.at[pair]
        )

    def kept_copy(pair):
        piece, place = tails[pair]
        return pltpu.make_async_copy(
            before[piece].at[place], later_refs[piece].at[place], later_sem.at[pair]
        )

    def each_later(act):
        for pair in range(len(tails)):
            link = entry("link", pair)
            pl.when(link >= 0)(lambda pair=pair: act(later_copy(pair)))
            if fresh:
                pl.when(link < 0)(lambda pair=pair: act(kept_copy(pair)))

    each_later(lambda copy: copy.start())
    for pair in range(pairs):
        pl.when(entry("final", pair) == 1)(lambda pair=pair: out_copy(pair).wait())
    each_later(lambda copy: copy.wait())


def piece_call(layout, number, table, lasts, part, held, out, later_parts, fresh):
    smem = pl.BlockSpec(memory_space=pltpu.SMEM)
    hbm = pl.BlockSpec(memory_space=pl.ANY)
    pairs, width = held.shape[0], held.shape[1]
    later = [value.shape[0] // 2 for value in later_parts]
    first_alias = 1 + len(lasts) + 2
    result = pl.pallas_call(
        functools.partial(piece_kernel, len(lasts), later, fresh, layout, number),
        out_shape=tuple(
            jax.ShapeDtypeStruct(value.shape, value.dtype) for value in (out, *later_parts)
        ),
        in_specs=[smem] + [hbm] * (len(lasts) + 3 + len(later)),
        out_specs=(hbm,) * (1 + len(later)),
        input_output_aliases={
            first_alias + place: place for place in range(1 if fresh else 1 + len(later))
        },
        scratch_shapes=[
            pltpu.VMEM(lasts[0].shape, lasts[0].dtype),
            pltpu.VMEM(part.shape, part.dtype),
            pltpu.VMEM(held.shape, held.dtype),
            pltpu.VMEM(part.shape, part.dtype),
            pltpu.VMEM(held.shape, held.dtype),
            pltpu.SemaphoreType.DMA((3,)),
            pltpu.SemaphoreType.DMA((pairs,)),
            pltpu.SemaphoreType.DMA((max(1, 2 * sum(later)),)),
        ],
        compiler_params=pltpu.CompilerParams(vmem_limit_bytes=PIECE_VMEM if fresh else VMEM_BYTES),
        cost_estimate=SMALL,
        name="last_panel_piece",
    )(table, *lasts, part, held, out, *later_parts)
    return result[0], list(result[1:])


def final_kernel(choices, layout, number, table_ref, *refs):
    lasts, refs = refs[:choices], refs[choices:]
    part_hbm, held, _, out_ref, part, products, staged, part_sem, out_sem = refs
    pairs = part.shape[0]
    part_copy = pltpu.make_async_copy(part_hbm, part, part_sem)
    part_copy.start()

    def entry(name, pair):
        return table_ref[layout[name, number] + pair]

    def out_copy(pair):
        return pltpu.make_async_copy(
            staged.at[pair], out_ref.at[entry("here", pair)], out_sem.at[pair]
        )

    flag = table_ref[layout["flags"]]
    for block in range(pairs // 2):
        left = lasts[0][block]
        for place in range(1, choices):
            left = jnp.where(flag == place, lasts[place][block], left)
        for pair in (2 * block, 2 * block + 1):
            products[pair] = jnp.dot(left, held[pair], preferred_element_type=jnp.float32)
    part_copy.wait()
    for pair in range(pairs):
        part[entry("lead", pair)] += products[pair]
    for pair in range(pairs):
        staged[pair] = part[entry("lead", pair)].astype(staged.dtype)
        pl.when(entry("final", pair) == 1)(lambda pair=pair: out_copy(pair).start())
    for pair in range(pairs):
        pl.when(entry("final", pair) == 1)(lambda pair=pair: out_copy(pair).wait())


def final_call(layout, number, table, lasts, part, held, out):
    smem = pl.BlockSpec(memory_space=pltpu.SMEM)
    vmem = pl.BlockSpec(memory_space=pltpu.VMEM)
    hbm = pl.BlockSpec(memory_space=pl.ANY)
    pinned = pl.BlockSpec(memory_space=pltpu.HBM)
    pairs, width = held.shape[0], held.shape[1]
    return pl.pallas_call(
        functools.partial(final_kernel, len(lasts), layout, number),
        out_shape=jax.ShapeDtypeStruct(out.shape, out.dtype),
        in_specs=[smem] + [vmem] * len(lasts) + [pinned, vmem, hbm],
        out_specs=hbm,
        input_output_aliases={len(lasts) + 3: 0},
        scratch_shapes=[
            pltpu.VMEM(part.shape, part.dtype),
            pltpu.VMEM(part.shape, part.dtype),
            pltpu.VMEM(held.shape, held.dtype),
            pltpu.SemaphoreType.DMA,
            pltpu.SemaphoreType.DMA((pairs,)),
        ],
        compiler_params=pltpu.CompilerParams(vmem_limit_bytes=FINAL_VMEM),
        cost_estimate=SMALL,
        name="last_piece",
    )(table, *lasts, part, held, out)


def cut(value, sizes):
    starts = [sum(sizes[:place]) for place in range(len(sizes))]
    return [value[start : start + size] for start, size in zip(starts, sizes)]


def after(value, *others):
    return lax.optimization_barrier((value, *others))[0]


def line_columns(me):
    low = me < 2
    return jnp.stack([me, me ^ 1, jnp.where(low, 2, 1), jnp.where(low, 3, 0)])


def ring_columns(me):
    return (me + jnp.arange(STEPS, dtype=jnp.int32)) % lax.axis_size("col")


def line_of_four(left, far_sizes, early, fetched):
    blocks = left.shape[0]
    cross, out = [(1, 2), (2, 1)], [(2, 3), (1, 0)]
    near = lax.ppermute(left, "col", [(0, 1), (1, 0), (2, 3), (3, 2)])
    mid_in = lax.ppermute(left, "col", cross)
    mid_out = lax.ppermute(mid_in, "col", out)
    near = after(near, mid_in, early)
    far_in = [
        lax.ppermute(after(piece, *fetched) if place == 1 else piece, "col", cross)
        for place, piece in enumerate(cut(near, far_sizes))
    ]
    far_out = [
        lax.ppermute(after(piece, mid_out) if place else piece, "col", out)
        for place, piece in enumerate(far_in)
    ]
    routes = [(0, 0, blocks, None), (1, blocks, blocks, None)]
    routes += [(2, 2 * blocks, blocks, 0), (2, 2 * blocks, blocks, 1)]
    return routes, [left, near, mid_in, mid_out], list(zip(far_in, far_out))


def ring(left, far_sizes, *_):
    blocks = left.shape[0]
    near = shifted(left, "col", -1)
    mid = shifted(near, "col", -1)
    far = [shifted(piece, "col", -1) for piece in cut(mid, far_sizes)]
    routes = [(step, step * blocks, blocks, None) for step in range(STEPS - 1)]
    return routes, [left, near, mid], [(piece,) for piece in far]


def right_panels(right):
    count = lax.axis_size("row")
    rows = range(count)

    def send(value, takers, distance):
        pairs = [((row + distance) % count, row) for row in rows if row % 4 in takers]
        return lax.ppermute(value, "row", pairs)

    own = send(right, (0, 2), 1)
    two = send(right, (0, 1, 2, 3), 2)
    three = send(right, (1, 3), 3)
    return own, two, three


def passed_on(own, two, three):
    half = two.shape[0] // 2
    rows = range(lax.axis_size("row"))
    swap = [(row, row ^ 1) for row in rows]
    passed = [lax.ppermute(part, "row", swap) for part in (two[:half], two[half:])]
    takers = [(1, 0, (0, 2)), (2, 0, (0, 1, 2, 3)), (3, 0, (1, 3))]
    for place in range(2):
        takers += [(1, place * half, (1, 3)), (3, place * half, (0, 2))]
    return takers, [own, two, three, *[part for part in passed for _ in range(2)]]


def pair_tables(columns, a_rows, a_inner, b_inner, b_cols, own_rows, own_cols):
    row_id, col_id = lax.axis_index("row"), lax.axis_index("col")
    row_count, col_count = lax.axis_size("row"), lax.axis_size("col")
    steps = (columns - col_id + col_count) % col_count
    left_rows, left_inner = a_rows[row_id][columns], a_inner[row_id][columns]
    right_rows = (row_id + steps) % row_count
    right_inner = b_inner[:, col_id][right_rows]
    right_cols = b_cols[:, col_id][right_rows]
    count = right_inner.shape[1]
    places = jnp.arange(count, dtype=jnp.int32)
    matches = left_inner[:, :, None] == right_inner[:, None, :]
    first = jnp.min(jnp.where(matches, places, count - 1), axis=2)
    second = jnp.max(jnp.where(matches, places, 0), axis=2)
    picks = jnp.stack([first, second], axis=2)
    pair_cols = jnp.sum(
        jnp.where(picks[..., None] == places, right_cols[:, None, None, :], 0), axis=3
    )
    hits = (left_rows[:, :, None, None] == own_rows) & (pair_cols[..., None] == own_cols)
    slot_places = jnp.arange(own_rows.shape[0], dtype=jnp.int32)
    slots = jnp.sum(jnp.where(hits, slot_places, 0), axis=3)
    picks = picks + (steps * count)[:, None, None]
    return picks.reshape(-1).astype(jnp.int32), slots.reshape(-1).astype(jnp.int32)


def piece_tables(slots, sizes):
    cuts = cut(slots, [2 * size for size in sizes])
    tables = {}
    for number, here in enumerate(cuts):
        count = here.shape[0]
        places = jnp.arange(count, dtype=jnp.int32)

        def lead(wanted):
            same = wanted[:, None] == here[None, :]
            first = jnp.min(jnp.where(same, places[None, :], count), axis=1)
            return jnp.where(first < count, first, -1)

        again = (here[:, None] == here[None, :]) & (places[None, :] > places[:, None])
        tables["here", number] = here
        tables["lead", number] = lead(here)
        tables["final", number] = 1 - jnp.max(again.astype(jnp.int32), axis=1)
        if number + 1 < len(sizes):
            tables["link", number] = lead(jnp.concatenate(cuts[number + 1 :]))
    return tables


def packed(tables):
    starts, total = {}, 0
    for name, value in tables.items():
        starts[name], total = total, total + value.shape[0]
    return jnp.concatenate([value.astype(jnp.int32) for value in tables.values()]), starts


def on_device(a_panels, b_panels, a_rows, a_inner, b_inner, b_cols, c_rows, c_cols):
    row_id, col_id = lax.axis_index("row"), lax.axis_index("col")
    left, right = a_panels[0, 0], b_panels[0, 0]
    own_rows, own_cols = c_rows[row_id, col_id], c_cols[row_id, col_id]
    on_line = lax.axis_size("col") == STEPS
    blocks = left.shape[0]
    far_sizes = (blocks // 2, blocks - blocks // 2 - 3 * blocks // 16, 3 * blocks // 16)
    columns = (line_columns if on_line else ring_columns)(col_id)
    picks, slots = pair_tables(columns, a_rows, a_inner, b_inner, b_cols, own_rows, own_cols)
    at_end = on_line & ((col_id == 0) | (col_id == 3))
    flags = jnp.stack([at_end.astype(jnp.int32), row_id % 4])
    pieces = piece_tables(slots[-2 * left.shape[0] :], far_sizes)
    table, layout = packed({"flags": flags, "picks": picks, "slots": slots, **pieces})
    gather = line_of_four if on_line else ring
    fetched = right_panels(right)
    routes, sources, lasts = gather(left, far_sizes, table, fetched)
    takers, rights = passed_on(*fetched)
    out, parts, helds = main_call(
        routes,
        [(0, 0, (0, 1, 2, 3)), *takers],
        far_sizes,
        layout,
        table,
        sources,
        [right, *rights],
        c_rows.shape[2],
    )
    last = len(far_sizes) - 1
    for number in range(last):
        out, parts[number + 1 :] = piece_call(
            layout, number, table, lasts[number], parts[number], helds[number], out, parts[number + 1 :], number == last - 1
        )
    out = final_call(layout, last, table, lasts[last], parts[last], helds[last], out)
    return out[None, None]


def solution(mesh):
    in_specs = (
        P("row", "col", None, None, None),
        P("row", "col", None, None, None),
        P(),
        P(),
        P(),
        P(),
        P(),
        P(),
    )
    out_specs = P("row", "col", None, None, None)
    return jax.shard_map(
        on_device, mesh=mesh, in_specs=in_specs, out_specs=out_specs, check_vma=False
    )
```

```python
import functools

import jax
import jax.numpy as jnp
from jax import lax
from jax.experimental import pallas as pl
from jax.experimental.pallas import tpu as pltpu
from jax.sharding import PartitionSpec as P

STEPS = 4
VMEM_BYTES = 60 * 2**20
PIECE_VMEM = 40 * 2**20
FINAL_VMEM = 16 * 2**20
UNROLL = 4
SMALL = pl.CostEstimate(flops=2**20, bytes_accessed=2**16, transcendentals=0)


def shifted(value, axis, steps):
    count = lax.axis_size(axis)
    pairs = [(source, (source + steps) % count) for source in range(count)]
    return lax.ppermute(value, axis, pairs)


def main_kernel(routes, takers, pieces, layout, table_ref, *refs):
    count = len(pieces)
    sources, refs = refs[: len(routes)], refs[len(routes) :]
    rights, refs = refs[: len(takers)], refs[len(takers) :]
    out_ref, part_refs, held_refs = refs[0], refs[1 : 1 + count], refs[1 + count : 1 + 2 * count]
    lefts, right_all, totals, staged, left_sem, right_sem, out_sem, part_sem, held_sem = refs[
        1 + 2 * count :
    ]
    blocks = rights[0].shape[0]
    slots = totals.shape[0]
    flag, kind = table_ref[layout["flags"]], table_ref[layout["flags"] + 1]

    def pick_of(pair):
        return table_ref[layout["picks"] + pair]

    def slot_of(pair):
        return table_ref[layout["slots"] + pair]

    def left_copy(place):
        _, start, size, _ = routes[place]
        return pltpu.make_async_copy(
            sources[place], lefts.at[pl.ds(start, size)], left_sem.at[place]
        )

    def when_used(place, action):
        wanted = routes[place][3]
        if wanted is None:
            action()
        else:
            pl.when(flag == wanted)(action)

    def right_copy(place):
        step, start, _ = takers[place]
        return pltpu.make_async_copy(
            rights[place],
            right_all.at[pl.ds(step * blocks + start, rights[place].shape[0])],
            right_sem.at[place],
        )

    def when_taken(step, action):
        for place, (wanted, _, kinds) in enumerate(takers):
            if wanted == step:
                for one in kinds:
                    pl.when(kind == one)(lambda place=place: action(place))

    for step in range(STEPS):
        for place, route in enumerate(routes):
            if route[0] == step:
                when_used(place, lambda place=place: left_copy(place).start())
        when_taken(step, lambda place: right_copy(place).start())

    @pl.loop(0, slots)
    def _(slot):
        totals[slot] = jnp.zeros(totals.shape[1:], totals.dtype)

    first_held = 2 * (STEPS - 1) * blocks
    tails = []
    for piece, size in enumerate(pieces):
        tails += [(piece, place) for place in range(2 * size)]

    def held_copy(pair):
        piece, place = tails[pair]
        return pltpu.make_async_copy(
            right_all.at[pick_of(first_held + pair)],
            held_refs[piece].at[place],
            held_sem.at[pair],
        )

    def part_copy(pair):
        piece, place = tails[pair]
        return pltpu.make_async_copy(
            totals.at[slot_of(first_held + pair)],
            part_refs[piece].at[place],
            part_sem.at[pair],
        )

    def out_copy(slot):
        return pltpu.make_async_copy(staged.at[slot], out_ref.at[slot], out_sem.at[slot])

    for step in range(STEPS - 1):
        for place, route in enumerate(routes):
            if route[0] == step:
                when_used(place, lambda place=place: left_copy(place).wait())
        for other in [(0,), range(1, STEPS), ()][min(step, 2)]:
            when_taken(other, lambda place: right_copy(place).wait())
        if step == 1:
            for pair in range(len(tails)):
                held_copy(pair).start()

        @pl.loop(step * blocks, (step + 1) * blocks, unroll=UNROLL)
        def _(left):
            for side in range(2):
                totals[slot_of(2 * left + side)] += jnp.dot(
                    lefts[left],
                    right_all[pick_of(2 * left + side)],
                    preferred_element_type=jnp.float32,
                )

    for pair in range(len(tails)):
        part_copy(pair).start()

    @pl.loop(0, slots)
    def _(slot):
        staged[slot] = totals[slot].astype(staged.dtype)
        out_copy(slot).start()

    @pl.loop(0, slots)
    def _(slot):
        out_copy(slot).wait()

    for pair in range(len(tails)):
        part_copy(pair).wait()
        held_copy(pair).wait()


def main_call(routes, takers, pieces, layout, table, sources, rights, slot_count):
    blocks, width = rights[0].shape[0], rights[0].shape[1]
    dtype = rights[0].dtype
    smem = pl.BlockSpec(memory_space=pltpu.SMEM)
    hbm = pl.BlockSpec(memory_space=pl.ANY)
    kept = (STEPS - 1) * blocks
    result = pl.pallas_call(
        functools.partial(main_kernel, routes, takers, pieces, layout),
        out_shape=(
            jax.ShapeDtypeStruct((slot_count, width, width), dtype),
            *[jax.ShapeDtypeStruct((2 * size, width, width), jnp.float32) for size in pieces],
            *[jax.ShapeDtypeStruct((2 * size, width, width), dtype) for size in pieces],
        ),
        in_specs=[smem] + [hbm] * (len(sources) + len(rights)),
        out_specs=(hbm,) * (1 + 2 * len(pieces)),
        scratch_shapes=[
            pltpu.VMEM((kept, width, width), dtype),
            pltpu.VMEM((STEPS * blocks, width, width), dtype),
            pltpu.VMEM((slot_count, width, width), jnp.float32),
            pltpu.VMEM((slot_count, width, width), dtype),
            pltpu.SemaphoreType.DMA((len(sources),)),
            pltpu.SemaphoreType.DMA((len(rights),)),
            pltpu.SemaphoreType.DMA((slot_count,)),
            pltpu.SemaphoreType.DMA((2 * blocks,)),
            pltpu.SemaphoreType.DMA((2 * blocks,)),
        ],
        compiler_params=pltpu.CompilerParams(vmem_limit_bytes=VMEM_BYTES),
        cost_estimate=SMALL,
        name="first_panels",
    )(table, *sources, *rights)
    return result[0], list(result[1 : 1 + len(pieces)]), list(result[1 + len(pieces) :])


def piece_kernel(choices, later, fresh, layout, number, table_ref, *refs):
    def entry(name, pair):
        return table_ref[layout[name, number] + pair]

    lasts, refs = refs[:choices], refs[choices:]
    part_hbm, held_hbm, before, refs = refs[0], refs[1], refs[3 : 3 + len(later)], refs[3 + len(later) :]
    out_ref, later_refs, refs = refs[0], refs[1 : 1 + len(later)], refs[1 + len(later) :]
    left, part, held, products, staged, in_sem, out_sem, later_sem = refs
    pairs = part.shape[0]

    left_copies = [pltpu.make_async_copy(last, left, in_sem.at[0]) for last in lasts]
    held_copy = pltpu.make_async_copy(held_hbm, held, in_sem.at[1])
    part_copy = pltpu.make_async_copy(part_hbm, part, in_sem.at[2])

    def out_copy(pair):
        return pltpu.make_async_copy(
            staged.at[pair], out_ref.at[entry("here", pair)], out_sem.at[pair]
        )

    held_copy.start()
    part_copy.start()
    for place, copy in enumerate(left_copies):
        pl.when(table_ref[layout["flags"]] == place)(copy.start)
    left_copies[0].wait()
    held_copy.wait()
    for pair in range(pairs):
        products[pair] = jnp.dot(
            left[pair // 2], held[pair], preferred_element_type=jnp.float32
        )
    part_copy.wait()
    for pair in range(pairs):
        part[entry("lead", pair)] += products[pair]
    for pair in range(pairs):
        staged[pair] = part[entry("lead", pair)].astype(staged.dtype)
        pl.when(entry("final", pair) == 1)(lambda pair=pair: out_copy(pair).start())

    tails = []
    for piece, size in enumerate(later):
        tails += [(piece, place) for place in range(2 * size)]

    def later_copy(pair):
        piece, place = tails[pair]
        return pltpu.make_async_copy(
            part.at[entry("link", pair)], later_refs[piece].at[place], later_sem.at[pair]
        )

    def kept_copy(pair):
        piece, place = tails[pair]
        return pltpu.make_async_copy(
            before[piece].at[place], later_refs[piece].at[place], later_sem.at[pair]
        )

    def each_later(act):
        for pair in range(len(tails)):
            link = entry("link", pair)
            pl.when(link >= 0)(lambda pair=pair: act(later_copy(pair)))
            if fresh:
                pl.when(link < 0)(lambda pair=pair: act(kept_copy(pair)))

    each_later(lambda copy: copy.start())
    for pair in range(pairs):
        pl.when(entry("final", pair) == 1)(lambda pair=pair: out_copy(pair).wait())
    each_later(lambda copy: copy.wait())


def piece_call(layout, number, table, lasts, part, held, out, later_parts, fresh):
    smem = pl.BlockSpec(memory_space=pltpu.SMEM)
    hbm = pl.BlockSpec(memory_space=pl.ANY)
    pairs, width = held.shape[0], held.shape[1]
    later = [value.shape[0] // 2 for value in later_parts]
    first_alias = 1 + len(lasts) + 2
    result = pl.pallas_call(
        functools.partial(piece_kernel, len(lasts), later, fresh, layout, number),
        out_shape=tuple(
            jax.ShapeDtypeStruct(value.shape, value.dtype) for value in (out, *later_parts)
        ),
        in_specs=[smem] + [hbm] * (len(lasts) + 3 + len(later)),
        out_specs=(hbm,) * (1 + len(later)),
        input_output_aliases={
            first_alias + place: place for place in range(1 if fresh else 1 + len(later))
        },
        scratch_shapes=[
            pltpu.VMEM(lasts[0].shape, lasts[0].dtype),
            pltpu.VMEM(part.shape, part.dtype),
            pltpu.VMEM(held.shape, held.dtype),
            pltpu.VMEM(part.shape, part.dtype),
            pltpu.VMEM(held.shape, held.dtype),
            pltpu.SemaphoreType.DMA((3,)),
            pltpu.SemaphoreType.DMA((pairs,)),
            pltpu.SemaphoreType.DMA((max(1, 2 * sum(later)),)),
        ],
        compiler_params=pltpu.CompilerParams(vmem_limit_bytes=PIECE_VMEM if fresh else VMEM_BYTES),
        cost_estimate=SMALL,
        name="last_panel_piece",
    )(table, *lasts, part, held, out, *later_parts)
    return result[0], list(result[1:])


def final_kernel(choices, layout, number, table_ref, *refs):
    lasts, refs = refs[:choices], refs[choices:]
    part_hbm, held, _, out_ref, part, products, staged, part_sem, out_sem = refs
    pairs = part.shape[0]
    part_copy = pltpu.make_async_copy(part_hbm, part, part_sem)
    part_copy.start()

    def entry(name, pair):
        return table_ref[layout[name, number] + pair]

    def out_copy(pair):
        return pltpu.make_async_copy(
            staged.at[pair], out_ref.at[entry("here", pair)], out_sem.at[pair]
        )

    flag = table_ref[layout["flags"]]
    for block in range(pairs // 2):
        left = lasts[0][block]
        for place in range(1, choices):
            left = jnp.where(flag == place, lasts[place][block], left)
        for pair in (2 * block, 2 * block + 1):
            products[pair] = jnp.dot(left, held[pair], preferred_element_type=jnp.float32)
    part_copy.wait()
    for pair in range(pairs):
        part[entry("lead", pair)] += products[pair]
    for pair in range(pairs):
        staged[pair] = part[entry("lead", pair)].astype(staged.dtype)
        pl.when(entry("final", pair) == 1)(lambda pair=pair: out_copy(pair).start())
    for pair in range(pairs):
        pl.when(entry("final", pair) == 1)(lambda pair=pair: out_copy(pair).wait())


def final_call(layout, number, table, lasts, part, held, out):
    smem = pl.BlockSpec(memory_space=pltpu.SMEM)
    vmem = pl.BlockSpec(memory_space=pltpu.VMEM)
    hbm = pl.BlockSpec(memory_space=pl.ANY)
    pinned = pl.BlockSpec(memory_space=pltpu.HBM)
    pairs, width = held.shape[0], held.shape[1]
    return pl.pallas_call(
        functools.partial(final_kernel, len(lasts), layout, number),
        out_shape=jax.ShapeDtypeStruct(out.shape, out.dtype),
        in_specs=[smem] + [vmem] * len(lasts) + [pinned, vmem, hbm],
        out_specs=hbm,
        input_output_aliases={len(lasts) + 3: 0},
        scratch_shapes=[
            pltpu.VMEM(part.shape, part.dtype),
            pltpu.VMEM(part.shape, part.dtype),
            pltpu.VMEM(held.shape, held.dtype),
            pltpu.SemaphoreType.DMA,
            pltpu.SemaphoreType.DMA((pairs,)),
        ],
        compiler_params=pltpu.CompilerParams(vmem_limit_bytes=FINAL_VMEM),
        cost_estimate=SMALL,
        name="last_piece",
    )(table, *lasts, part, held, out)


def cut(value, sizes):
    starts = [sum(sizes[:place]) for place in range(len(sizes))]
    return [value[start : start + size] for start, size in zip(starts, sizes)]


def after(value, *others):
    return lax.optimization_barrier((value, *others))[0]


def line_columns(me):
    low = me < 2
    return jnp.stack([me, me ^ 1, jnp.where(low, 2, 1), jnp.where(low, 3, 0)])


def ring_columns(me):
    return (me + jnp.arange(STEPS, dtype=jnp.int32)) % lax.axis_size("col")


def line_of_four(left, far_sizes, early, fetched):
    blocks = left.shape[0]
    cross, out = [(1, 2), (2, 1)], [(2, 3), (1, 0)]
    near = lax.ppermute(left, "col", [(0, 1), (1, 0), (2, 3), (3, 2)])
    mid_in = lax.ppermute(left, "col", cross)
    mid_out = lax.ppermute(mid_in, "col", out)
    near = after(near, mid_in, early)
    far_in = [
        lax.ppermute(after(piece, *fetched) if place == 1 else piece, "col", cross)
        for place, piece in enumerate(cut(near, far_sizes))
    ]
    far_out = [
        lax.ppermute(after(piece, mid_out) if place else piece, "col", out)
        for place, piece in enumerate(far_in)
    ]
    routes = [(0, 0, blocks, None), (1, blocks, blocks, None)]
    routes += [(2, 2 * blocks, blocks, 0), (2, 2 * blocks, blocks, 1)]
    return routes, [left, near, mid_in, mid_out], list(zip(far_in, far_out))


def ring(left, far_sizes, *_):
    blocks = left.shape[0]
    near = shifted(left, "col", -1)
    mid = shifted(near, "col", -1)
    far = [shifted(piece, "col", -1) for piece in cut(mid, far_sizes)]
    routes = [(step, step * blocks, blocks, None) for step in range(STEPS - 1)]
    return routes, [left, near, mid], [(piece,) for piece in far]


def right_panels(right):
    count = lax.axis_size("row")
    rows = range(count)

    def send(value, takers, distance):
        pairs = [((row + distance) % count, row) for row in rows if row % 4 in takers]
        return lax.ppermute(value, "row", pairs)

    own = send(right, (0, 2), 1)
    two = send(right, (0, 1, 2, 3), 2)
    three = send(right, (1, 3), 3)
    return own, two, three


def passed_on(own, two, three):
    half = two.shape[0] // 2
    rows = range(lax.axis_size("row"))
    swap = [(row, row ^ 1) for row in rows]
    passed = [lax.ppermute(part, "row", swap) for part in (two[:half], two[half:])]
    takers = [(1, 0, (0, 2)), (2, 0, (0, 1, 2, 3)), (3, 0, (1, 3))]
    for place in range(2):
        takers += [(1, place * half, (1, 3)), (3, place * half, (0, 2))]
    return takers, [own, two, three, *[part for part in passed for _ in range(2)]]


def pair_tables(columns, a_rows, a_inner, b_inner, b_cols, own_rows, own_cols):
    row_id, col_id = lax.axis_index("row"), lax.axis_index("col")
    row_count, col_count = lax.axis_size("row"), lax.axis_size("col")
    steps = (columns - col_id + col_count) % col_count
    left_rows, left_inner = a_rows[row_id][columns], a_inner[row_id][columns]
    right_rows = (row_id + steps) % row_count
    right_inner = b_inner[:, col_id][right_rows]
    right_cols = b_cols[:, col_id][right_rows]
    count = right_inner.shape[1]
    places = jnp.arange(count, dtype=jnp.int32)
    matches = left_inner[:, :, None] == right_inner[:, None, :]
    first = jnp.min(jnp.where(matches, places, count - 1), axis=2)
    second = jnp.max(jnp.where(matches, places, 0), axis=2)
    picks = jnp.stack([first, second], axis=2)
    pair_cols = jnp.sum(
        jnp.where(picks[..., None] == places, right_cols[:, None, None, :], 0), axis=3
    )
    hits = (left_rows[:, :, None, None] == own_rows) & (pair_cols[..., None] == own_cols)
    slot_places = jnp.arange(own_rows.shape[0], dtype=jnp.int32)
    slots = jnp.sum(jnp.where(hits, slot_places, 0), axis=3)
    picks = picks + (steps * count)[:, None, None]
    return picks.reshape(-1).astype(jnp.int32), slots.reshape(-1).astype(jnp.int32)


def piece_tables(slots, sizes):
    cuts = cut(slots, [2 * size for size in sizes])
    tables = {}
    for number, here in enumerate(cuts):
        count = here.shape[0]
        places = jnp.arange(count, dtype=jnp.int32)

        def lead(wanted):
            same = wanted[:, None] == here[None, :]
            first = jnp.min(jnp.where(same, places[None, :], count), axis=1)
            return jnp.where(first < count, first, -1)

        again = (here[:, None] == here[None, :]) & (places[None, :] > places[:, None])
        tables["here", number] = here
        tables["lead", number] = lead(here)
        tables["final", number] = 1 - jnp.max(again.astype(jnp.int32), axis=1)
        if number + 1 < len(sizes):
            tables["link", number] = lead(jnp.concatenate(cuts[number + 1 :]))
    return tables


def packed(tables):
    starts, total = {}, 0
    for name, value in tables.items():
        starts[name], total = total, total + value.shape[0]
    return jnp.concatenate([value.astype(jnp.int32) for value in tables.values()]), starts


def on_device(a_panels, b_panels, a_rows, a_inner, b_inner, b_cols, c_rows, c_cols):
    row_id, col_id = lax.axis_index("row"), lax.axis_index("col")
    left, right = a_panels[0, 0], b_panels[0, 0]
    own_rows, own_cols = c_rows[row_id, col_id], c_cols[row_id, col_id]
    on_line = lax.axis_size("col") == STEPS
    blocks = left.shape[0]
    far_sizes = (blocks - 2 * (blocks // 4), blocks // 4, blocks // 4 - blocks // 8, blocks // 8)
    columns = (line_columns if on_line else ring_columns)(col_id)
    picks, slots = pair_tables(columns, a_rows, a_inner, b_inner, b_cols, own_rows, own_cols)
    at_end = on_line & ((col_id == 0) | (col_id == 3))
    flags = jnp.stack([at_end.astype(jnp.int32), row_id % 4])
    pieces = piece_tables(slots[-2 * left.shape[0] :], far_sizes)
    table, layout = packed({"flags": flags, "picks": picks, "slots": slots, **pieces})
    gather = line_of_four if on_line else ring
    fetched = right_panels(right)
    routes, sources, lasts = gather(left, far_sizes, table, fetched)
    takers, rights = passed_on(*fetched)
    out, parts, helds = main_call(
        routes,
        [(0, 0, (0, 1, 2, 3)), *takers],
        far_sizes,
        layout,
        table,
        sources,
        [right, *rights],
        c_rows.shape[2],
    )
    last = len(far_sizes) - 1
    for number in range(last):
        out, parts[number + 1 :] = piece_call(
            layout, number, table, lasts[number], parts[number], helds[number], out, parts[number + 1 :], number == last - 1
        )
    out = final_call(layout, last, table, lasts[last], parts[last], helds[last], out)
    return out[None, None]


def solution(mesh):
    in_specs = (
        P("row", "col", None, None, None),
        P("row", "col", None, None, None),
        P(),
        P(),
        P(),
        P(),
        P(),
        P(),
    )
    out_specs = P("row", "col", None, None, None)
    return jax.shard_map(
        on_device, mesh=mesh, in_specs=in_specs, out_specs=out_specs, check_vma=False
    )
```
